256 devices in a mesh: space: 32 (over x, z_hi, core), chan: 8 (over z_lo, y).
Axes of the slice: x: 4, y: 4, z: 8 (z_hi: 4, z_lo: 2; z = z_hi * 2 + z_lo), core: 2. Of those that a mesh axis runs over, the one named last changes fastest.
Arguments:
- features: bfloat16 [64, 16, 16, 1024], P('space', None, None, 'chan'), may hold values from -6 to 6
- slot_tile: int32 [64], replicated, may hold values from 0 to 63, as said below
- land: int32 [64], replicated, may hold values 0 or 1
- dw_kernel: float32 [7, 7, 1024], P(None, None, 'chan'), may hold values from -0.875 to 0.875
- dw_bias: float32 [1024], P('chan'), may hold values from -3 to 3
- ln_gain: float32 [1024], replicated, may hold values from 0.1 to 1.9
- ln_bias: float32 [1024], replicated, may hold values from -3 to 3
- w_in: bfloat16 [1024, 4096], P('space', 'chan'), may hold values from -0.1875 to 0.1875
- b_in: float32 [4096], P('chan'), may hold values from -3 to 3
- w_out: bfloat16 [4096, 1024], P('chan', 'space'), may hold values from -0.09375 to 0.09375
- b_out: float32 [1024], P('chan'), may hold values from -3 to 3
- layer_scale: float32 [1024], P('chan'), may hold values from 0.5 to 1.5
- cotangent: bfloat16 [64, 16, 16, 1024], P('space', None, None, 'chan'), may hold values from -0.1875 to 0.1875
Outputs:
- output: bfloat16 [64, 16, 16, 1024], P('space', None, None, 'chan')
- grad_in_weight: float32 [1024, 4096], P('space', 'chan')
- grad_out_weight: float32 [4096, 1024], P('chan', 'space')
The draws below stay inside these ranges and needn't reach their ends.
Inputs may be any that keep to these rules, and one draw needn't show every extreme that they name: slot_tile holds each band tile number once.
All inputs are finite; a program needn't handle non-finite values.
Results may differ from the reference program's by a relative error of at most 0.0071.
Values may be sent and summed in bfloat16 or wider, within the bound.
A program may use at most 64 MiB of HBM per device.

```python
import jax
import jax.numpy as jnp
from jax import lax

C = 1024
FF = 4096
TH = 16
TW = 16
TILES_DEV = 2
NT = 64


def draw_slot_tile(key, part):
    key = jax.random.fold_in(key, 11)
    first_key, second_key = jax.random.split(key)
    devices_all = NT // TILES_DEV
    half_count = devices_all // 2
    start_at = jax.random.randint(first_key, (), 0, half_count).astype(jnp.int32)
    positions = jnp.arange(devices_all, dtype=jnp.int32)
    pair_ids = positions // 2
    base_dev = (start_at + pair_ids) % half_count
    upper = (positions % 2 + pair_ids % 2) % 2
    device_of = base_dev + upper * half_count
    scores = jax.random.randint(second_key, (devices_all, TILES_DEV), 0, 1 << 20).astype(jnp.int32) * TILES_DEV + jnp.arange(TILES_DEV, dtype=jnp.int32)[None, :]
    within = jnp.argsort(jnp.argsort(scores, axis=1), axis=1).astype(jnp.int32)
    band_ids = jnp.arange(NT, dtype=jnp.int32)
    rounds = band_ids // devices_all
    owners = device_of[band_ids % devices_all]
    slot_ids = owners * TILES_DEV + within[owners, rounds]
    return jnp.zeros((NT,), jnp.int32).at[slot_ids].set(band_ids)


def set_ends(values, stream_key, least, largest):
    index_at = [jax.random.randint(jax.random.fold_in(stream_key, axis), (), 0, length) for axis, length in enumerate(values.shape)]
    main_axis = values.shape.index(max(values.shape))
    beside = index_at[:main_axis] + [(index_at[main_axis] + 1) % values.shape[main_axis]] + index_at[main_axis + 1:]
    return values.at[tuple(index_at)].set(least).at[tuple(beside)].set(largest)


def level_of(rng, extent, cuts, least, top_value):
    def one(axis_at, blocks):
        heights = jax.random.uniform(jax.random.fold_in(jax.random.fold_in(rng, 6), axis_at), (blocks,), jnp.float32, least / len(cuts), top_value / len(cuts))
        return jnp.repeat(jnp.exp(heights), extent[axis_at] // blocks).reshape((-1,) + (1,) * (len(extent) - axis_at - 1))

    level = one(*cuts[0])
    for cut in cuts[1:]:
        level = level * one(*cut)
    return level


def bell_draw(stream_key, dims, scale, most, shards=(), kind=jnp.bfloat16):
    loudness = level_of(stream_key, dims, shards, -0.22, 0.18) if shards else 1.0
    array = jax.random.normal(stream_key, dims, jnp.float32) * scale * loudness
    return jnp.minimum(jnp.maximum(array, -most), most).astype(kind)


def setup_inputs(seed: int = 0) -> dict:
    key_list = jax.random.split(jax.random.key(seed), 14)
    features = bell_draw(key_list[0], (NT, TH, TW, C), 1.0, 6.0, ((0, 32), (3, 8)))
    slot_tile = draw_slot_tile(jax.random.fold_in(key_list[13], 71), 0)
    land = set_ends((jax.random.randint(key_list[2], (NT,), 0, 5) < 3).astype(jnp.int32), jax.random.fold_in(key_list[2], 1), 0, 1)
    dw_kernel = bell_draw(key_list[3], (7, 7, C), 49 ** -0.5, 0.875, ((2, 8),), jnp.float32)
    dw_bias = bell_draw(key_list[4], (C,), 0.5, 3.0, ((0, 8),), jnp.float32)
    ln_gain = jnp.clip(1.0 + 0.18 * jax.random.normal(key_list[5], (C,), jnp.float32), 0.1, 1.9)
    ln_bias = bell_draw(key_list[6], (C,), 0.5, 3.0, (), jnp.float32)
    w_in = bell_draw(key_list[7], (C, FF), C ** -0.5, 0.1875, ((0, 32), (1, 8)))
    b_in = bell_draw(key_list[8], (FF,), 0.5, 3.0, ((0, 8),), jnp.float32)
    w_out = bell_draw(key_list[9], (FF, C), FF ** -0.5, 0.09375, ((0, 8), (1, 32)))
    b_out = bell_draw(key_list[10], (C,), 0.5, 3.0, ((0, 8),), jnp.float32)
    layer_scale = jnp.clip(0.5 + 1.0 * jax.random.uniform(key_list[11], (C,), jnp.float32) ** level_of(key_list[11], (C,), ((0, 8),), -0.2, 0.2), 0.5, 1.5)
    cotangent = bell_draw(key_list[12], (NT, TH, TW, C), (4.0 / (NT * TH * TW) ** 0.5), 0.1875, ((0, 32), (3, 8)))
    return dict(features=features, slot_tile=slot_tile, land=land, dw_kernel=dw_kernel, dw_bias=dw_bias, ln_gain=ln_gain, ln_bias=ln_bias, w_in=w_in, b_in=b_in, w_out=w_out, b_out=b_out, layer_scale=layer_scale, cotangent=cotangent)


def gelu_exact(values):
    return 0.5 * values * (1.0 + jax.scipy.special.erf(values * 0.7071067811865476))

def gelu_slope(values):
    return 0.5 * (1.0 + jax.scipy.special.erf(values * 0.7071067811865476)) + values * jnp.exp(-0.5 * values * values) * 0.3989422804014327

def layer_norm(rows, gain, shift):
    wide = rows.astype(jnp.float32)
    average = lax.optimization_barrier(jnp.mean(wide, axis=-1, keepdims=True))
    centered = wide - average
    spread = lax.optimization_barrier(jnp.mean(centered * centered, axis=-1, keepdims=True))
    return (centered * lax.rsqrt(spread + 1e-06) * gain.astype(jnp.float32) + shift.astype(jnp.float32)).astype(jnp.bfloat16)

def reference(features, slot_tile, land, dw_kernel, dw_bias, ln_gain, ln_bias, w_in, b_in, w_out, b_out, layer_scale, cotangent):
    tiles = features.shape[0]
    slot_land = land[slot_tile].astype(jnp.float32)[:, None, None, None]
    masked = features.astype(jnp.float32) * slot_land
    inverse = jnp.zeros((tiles,), jnp.int32).at[slot_tile].set(jnp.arange(tiles, dtype=jnp.int32))
    band = masked[inverse].transpose(1, 0, 2, 3).reshape(TH, tiles * TW, C)
    padded = jnp.pad(band, ((3, 3), (3, 3), (0, 0)))
    kernel = dw_kernel.astype(jnp.float32)
    conv = jnp.zeros((TH, tiles * TW, C), jnp.float32)
    for row in range(7):
        for col in range(7):
            conv = conv + kernel[row, col] * padded[row:row + TH, col:col + tiles * TW, :]
    dconv = (conv + dw_bias.astype(jnp.float32)).astype(jnp.bfloat16)
    slotted = dconv.reshape(TH, tiles, TW, C).transpose(1, 0, 2, 3)[slot_tile]
    normed = layer_norm(slotted.reshape(-1, C), ln_gain, ln_bias)
    pre = jnp.dot(normed, w_in, preferred_element_type=jnp.float32) + b_in.astype(jnp.float32)
    hidden = gelu_exact(pre).astype(jnp.bfloat16)
    mixed = jnp.dot(hidden, w_out, preferred_element_type=jnp.float32)
    row_land = jnp.broadcast_to(slot_land, (tiles, TH, TW, 1)).reshape(-1, 1)
    scale = layer_scale.astype(jnp.float32)
    output = (row_land * (features.reshape(-1, C).astype(jnp.float32) + scale * (mixed + b_out.astype(jnp.float32)))).astype(jnp.bfloat16)
    slope = (cotangent.reshape(-1, C).astype(jnp.float32) * row_land * scale).astype(jnp.bfloat16)
    grad_out_weight = jnp.dot(hidden.T, slope, preferred_element_type=jnp.float32)
    back = (jnp.dot(slope, w_out.T, preferred_element_type=jnp.float32) * gelu_slope(pre)).astype(jnp.bfloat16)
    grad_in_weight = jnp.dot(normed.T, back, preferred_element_type=jnp.float32)
    return (output.reshape(features.shape), grad_in_weight, grad_out_weight)
```

```python
import jax
import jax.numpy as jnp
from jax import lax
from jax.experimental import pallas as pl
from jax.experimental.pallas import tpu as pltpu
from jax.sharding import PartitionSpec as P

MESH = pl.DeviceIdType.MESH
F32, BF16 = jnp.float32, jnp.bfloat16
FAR = (1, 3, 2)
COPIES = 110


def wrap4(value):
    return lax.rem(value + 4, 4)


class Place:
    def __init__(self):
        self.space, self.chan = lax.axis_index("space"), lax.axis_index("chan")
        self.x, self.zh, self.core = self.space // 8, (self.space // 2) % 4, self.space % 2
        self.zl, self.y = self.chan // 4, self.chan % 4

    def slot(self, dx=0, dz=0, other=False):
        core = 1 - self.core if other else self.core
        return wrap4(self.x + dx) * 8 + wrap4(self.zh + dz) * 2 + core

    def part(self, dy=0, other=False):
        return (1 - self.zl if other else self.zl) * 4 + wrap4(self.y + dy)

    def peers(self):
        ids = [(self.slot(dz=d), self.chan) for d in (1, 2, 3)]
        ids += [(self.slot(dx=d), self.chan) for d in (1, 2, 3)]
        ids += [(self.slot(other=True), self.chan), (self.space, self.part(other=True))]
        return ids + [(self.space, self.part(dy=d)) for d in (1, 2, 3)]


class Links:
    def __init__(self, send_sems, recv_sems):
        self.send_sems, self.recv_sems, self.sent = send_sems, recv_sems, []

    def describe(self, number, source, target, device):
        return pltpu.make_async_remote_copy(
            src_ref=source,
            dst_ref=target,
            send_sem=self.send_sems.at[number],
            recv_sem=self.recv_sems.at[number],
            device_id=device,
            device_id_type=MESH,
        )

    def start(self, source, target, device):
        number = len(self.sent)
        assert number < COPIES
        copy = self.describe(number, source, target, device)
        copy.start()
        self.sent.append(copy)
        return number, device

    def landed(self, ticket, where):
        self.describe(ticket[0], where, where, ticket[1]).wait_recv()

    def finish(self):
        for copy in self.sent:
            copy.wait_send()


class SpaceGather:
    def __init__(self, links, place, block, use=lambda s: None):
        self.links, self.place, self.block, self.use = links, place, block, use
        self.over_z, self.over_x, self.over_core = {}, {}, {}

    def send(self, block, device):
        return self.links.start(block, block, device)

    def own_z(self):
        place = self.place
        mine = self.block(place.slot())
        for d in FAR:
            self.over_z[d] = self.send(mine, (place.slot(dz=d), place.chan))

    def spread(self, d):
        place = self.place
        block = self.block(place.slot(dz=-d))
        if d:
            self.links.landed(self.over_z[d], block)
        for e in FAR:
            self.over_x[d, e] = self.send(block, (place.slot(dx=e), place.chan))
        self.over_core[d, 0] = self.send(block, (place.slot(other=True), place.chan))
        self.use(place.slot(dz=-d))

    def cross(self, d, e):
        place = self.place
        block = self.block(place.slot(dx=-e, dz=-d))
        self.links.landed(self.over_x[d, e], block)
        self.over_core[d, e] = self.send(block, (place.slot(other=True), place.chan))
        self.use(place.slot(dx=-e, dz=-d))

    def wait(self):
        place = self.place
        for (d, e), ticket in self.over_core.items():
            self.links.landed(ticket, self.block(place.slot(dx=-e, dz=-d, other=True)))
            self.use(place.slot(dx=-e, dz=-d, other=True))


class ChanGather:
    def __init__(self, links, place, block):
        self.links, self.place, self.block = links, place, block
        self.over_y = {}

    def own(self):
        place = self.place
        mine = self.block(place.part())
        self.over_zl = self.links.start(mine, mine, (place.space, place.part(other=True)))
        self.spread(mine, False)

    def spread(self, block, other):
        place = self.place
        for d in FAR:
            self.over_y[d, other] = self.links.start(block, block, (place.space, place.part(dy=d)))

    def cross(self):
        block = self.block(self.place.part(other=True))
        self.links.landed(self.over_zl, block)
        self.spread(block, True)

    def wait(self):
        for (d, other), ticket in self.over_y.items():
            self.links.landed(ticket, self.block(self.place.part(dy=-d, other=other)))


def kernel(
    slot_tile, land, feat, cot, dw, dw_bias, gain, shift, w_in, b_in, w_out, b_out, scale,
    out, gin, gout,
    xpad, hbuf, hacc, wbuf, sbuf, cbuf, dbuf0, dbuf1, nbuf, pre, qbuf, hid, back,
    gacc, gsend, gcore, gxs, gxr, gown, gzs, gzr, msend, mrecv, mown, mzs, mzr,
    send_sems, recv_sems,
):
    place, links = Place(), Links(send_sems, recv_sems)
    core, zl = place.core, place.zl
    first = place.space * 2

    xpad[...] = jnp.zeros_like(xpad)
    tiles = [slot_tile[first + t] for t in range(2)]
    lands = [land[tile].astype(F32) for tile in tiles]
    for t in range(2):
        masked = feat[t * 256 : (t + 1) * 256, :].astype(F32) * lands[t]
        xpad[t, 3:19, 8:24, :] = masked.reshape(16, 16, 128)
        for side, begin in ((0, 0), (1, 13)):
            for q in range(3):
                column = xpad[t, 3:19, 8 + begin + q, :]
                hbuf[first * 2 + t * 2 + side, q] = column.astype(BF16)
    for t in range(2):
        rows = slice(t * 256, (t + 1) * 256)
        sbuf[place.chan, rows] = (cot[rows, :].astype(F32) * lands[t] * scale[...]).astype(BF16)
    wbuf[place.space, 0] = w_in[...]
    wide = jnp.concatenate((w_out[...].astype(F32), jnp.zeros((512, 96), F32)), axis=1)
    wbuf[place.space, 1] = wide.T[:32].astype(BF16)
    barrier = pltpu.get_barrier_semaphore()
    for peer in place.peers():
        pl.semaphore_signal(barrier, inc=1, device_id=peer, device_id_type=MESH)
    pl.semaphore_wait(barrier, len(place.peers()))

    hacc[...] = jnp.zeros((2, 2, 3, 16, 128), F32)

    def pick(s):
        held = [slot_tile[s * 2 + i] for i in range(2)]
        for t in range(2):
            for side, step in ((0, -1), (1, 1)):
                for i in range(2):
                    chosen = (held[i] == tiles[t] + step).astype(F32)
                    hacc[t, side] += hbuf[s * 4 + i * 2 + 1 - side].astype(F32) * chosen

    halos = SpaceGather(links, place, lambda s: hbuf.at[pl.ds(s * 4, 4)], pick)
    weights = SpaceGather(links, place, lambda s: wbuf.at[s])
    slopes = ChanGather(links, place, lambda c: sbuf.at[c])
    dbufs = (dbuf0, dbuf1)
    convs = [ChanGather(links, place, lambda c, held=held: held.at[c]) for held in dbufs]

    halos.own_z()
    halos.spread(0)
    slopes.own()

    for d in FAR:
        halos.spread(d)
    slopes.cross()
    weights.own_z()
    for d in (0,) + FAR:
        for e in FAR:
            halos.cross(d, e)
    weights.spread(0)
    halos.wait()

    for t in range(2):
        for q in range(3):
            xpad[t, 3:19, 5 + q, :] = hacc[t, 0, q]
            xpad[t, 3:19, 24 + q, :] = hacc[t, 1, q]
    for t in range(2):

        def half(h, carry):
            total = jnp.zeros((8, 16, 128), F32)
            for e in range(7):
                rows = xpad[t, pl.ds(h * 8, 14), 5 + e : 21 + e, :]
                for a in range(7):
                    total = total + dw[a, e : e + 1, :][None] * rows[a : a + 8]
            total = total + dw_bias[...][None]
            cbuf[t, pl.ds(pl.multiple_of(h * 128, 128), 128)] = total.reshape(128, 128).astype(BF16)
            return carry

        lax.fori_loop(0, 2, half, 0)
        dbufs[t][place.chan] = cbuf[t]
        convs[t].own()

    for d in FAR:
        weights.spread(d)
    convs[0].cross()
    convs[1].cross()
    for d in (0,) + FAR:
        for e in FAR:
            weights.cross(d, e)
    slopes.wait()
    weights.wait()

    for t in range(2):
        rows = slice(t * 256, (t + 1) * 256)
        slope_rows = jnp.concatenate([sbuf[c, rows] for c in range(8)], axis=1)
        qbuf[rows] = jnp.dot(
            slope_rows, wbuf[:, 1].reshape(1024, 512), preferred_element_type=F32
        )

    for t in range(2):
        convs[t].wait()

        def norm(i, carry):
            at = pl.ds(pl.multiple_of(i * 64, 64), 64)
            x = dbufs[t][:, at, :].astype(F32)
            mean = jnp.sum(jnp.sum(x, axis=0), axis=1, keepdims=True) * (1.0 / 1024)
            x = x - mean[None]
            spread = jnp.sum(jnp.sum(x * x, axis=0), axis=1, keepdims=True) * (1.0 / 1024)
            x = x * lax.rsqrt(spread + 1e-06)[None]
            to = pl.ds(pl.multiple_of(t * 256 + i * 64, 64), 64)
            for c in range(8):
                y = x[c] * gain[c : c + 1] + shift[c : c + 1]
                nbuf[to, c * 128 : (c + 1) * 128] = y.astype(BF16)
            return carry

        lax.fori_loop(0, 4, norm, 0)
        rows = slice(t * 256, (t + 1) * 256)
        pre[...] = (
            jnp.dot(nbuf[rows], wbuf[:, 0].reshape(1024, 512), preferred_element_type=F32)
            + b_in[...]
        )

        def act(i, carry):
            at = pl.ds(pl.multiple_of(i * 32, 32), 32)
            to = pl.ds(pl.multiple_of(t * 256 + i * 32, 32), 32)
            p = pre[at]
            below = 0.5 * (1.0 + lax.erf(p * 0.7071067811865476))
            hid[to] = (p * below).astype(BF16)
            rise = below + p * jnp.exp(-0.5 * p * p) * 0.3989422804014327
            back[to] = (qbuf[to] * rise).astype(BF16)
            return carry

        lax.fori_loop(0, 8, act, 0)

    over_core = {}
    for g in (1, 0):
        for i in range(4):
            if g:
                left = jnp.concatenate((sbuf[2 * i], sbuf[2 * i + 1]), axis=1)
            else:
                left = nbuf[:, i * 256 : (i + 1) * 256]
            summed = lax.dot_general(
                left, (hid if g else back)[...], (((0,), (0,)), ((), ())),
                preferred_element_type=F32,
            )
            gacc[g, 4 * i : 4 * i + 4] = summed.reshape(4, 2, 32, 512)
            gsend[g, 4 * i : 4 * i + 4] = gacc[g, 4 * i : 4 * i + 4, 1 - core].astype(BF16)
        over_core[g] = links.start(
            gsend.at[g], gcore.at[g], (place.slot(other=True), place.chan)
        )

    mixed_y = {}
    for d in FAR + (0,):
        to = wrap4(place.y + d)
        columns = jnp.concatenate(
            [wbuf[pl.ds(k * 16 + to * 4, 4), 1].reshape(128, 512) for k in range(2)], axis=0
        )
        partial = lax.dot_general(
            hid[...], columns, (((1,), (1,)), ((), ())), preferred_element_type=F32
        )
        for k in range(2):
            piece = partial[:, k * 128 : (k + 1) * 128]
            if d:
                msend[d - 1, k] = piece.astype(BF16)
            else:
                mown[k] = piece
        if d:
            mixed_y[d] = links.start(
                msend.at[d - 1], mrecv.at[d - 1], (place.space, place.part(dy=d))
            )

    over_x, over_z = {}, {}
    for g in (1, 0):
        links.landed(over_core[g], gcore.at[g])
        for d in FAR:
            at = pl.ds(wrap4(place.x + d) * 4, 4)
            gxs[g, d - 1] = (gacc[g, at, core] + gcore[g, at].astype(F32)).astype(BF16)
            over_x[g, d] = links.start(
                gxs.at[g, d - 1], gxr.at[g, d - 1], (place.slot(dx=d), place.chan)
            )
    for d in FAR:
        links.landed(mixed_y[d], mrecv.at[d - 1])
    for d in FAR:
        mown[...] += mrecv[d - 1].astype(F32)
    mzs[...] = mown[1 - zl].astype(BF16)
    mixed_z = links.start(mzs, mzr, (place.space, place.part(other=True)))
    for g in (1, 0):
        at = pl.ds(place.x * 4, 4)
        gown[g] = gacc[g, at, core] + gcore[g, at].astype(F32)
        for d in FAR:
            links.landed(over_x[g, d], gxr.at[g, d - 1])
            gown[g] += gxr[g, d - 1].astype(F32)
        for d in FAR:
            gzs[g, d - 1] = gown[g, wrap4(place.zh + d)].astype(BF16)
            over_z[g, d] = links.start(
                gzs.at[g, d - 1], gzr.at[g, d - 1], (place.slot(dz=d), place.chan)
            )
    links.landed(mixed_z, mzr)
    for t in range(2):
        rows = slice(t * 256, (t + 1) * 256)
        mixed = mown[zl, rows] + mzr[rows].astype(F32)
        value = feat[rows, :].astype(F32) + scale[...] * (mixed + b_out[...])
        out[rows, :] = (lands[t] * value).astype(BF16)
    for g, result in ((1, gout), (0, gin)):
        total = gown[g, place.zh]
        for d in FAR:
            links.landed(over_z[g, d], gzr.at[g, d - 1])
            total = total + gzr[g, d - 1].astype(F32)
        result[...] = total
    links.finish()


def body(
    features, slot_tile, land, dw_kernel, dw_bias, ln_gain, ln_bias, w_in, b_in, w_out, b_out,
    layer_scale, cotangent,
):
    vmem = pl.BlockSpec(memory_space=pltpu.VMEM)
    smem = pl.BlockSpec(memory_space=pltpu.SMEM)
    scratch = [
        ((2, 22, 32, 128), F32),
        ((128, 3, 16, 128), BF16),
        ((2, 2, 3, 16, 128), F32),
        ((32, 2, 32, 512), BF16),
        ((8, 512, 128), BF16),
        ((2, 256, 128), BF16),
        ((8, 256, 128), BF16),
        ((8, 256, 128), BF16),
        ((512, 1024), BF16),
        ((256, 512), F32),
        ((512, 512), F32),
        ((512, 512), BF16),
        ((512, 512), BF16),
        ((2, 16, 2, 32, 512), F32),
        ((2, 16, 32, 512), BF16),
        ((2, 16, 32, 512), BF16),
        ((2, 3, 4, 32, 512), BF16),
        ((2, 3, 4, 32, 512), BF16),
        ((2, 4, 32, 512), F32),
        ((2, 3, 32, 512), BF16),
        ((2, 3, 32, 512), BF16),
        ((3, 2, 512, 128), BF16),
        ((3, 2, 512, 128), BF16),
        ((2, 512, 128), F32),
        ((512, 128), BF16),
        ((512, 128), BF16),
    ]
    output, grad_in, grad_out = pl.pallas_call(
        kernel,
        out_shape=(
            jax.ShapeDtypeStruct((512, 128), BF16),
            jax.ShapeDtypeStruct((32, 512), F32),
            jax.ShapeDtypeStruct((32, 512), F32),
        ),
        in_specs=[smem, smem] + [vmem] * 11,
        out_specs=(vmem, vmem, vmem),
        scratch_shapes=[pltpu.VMEM(shape, dtype) for shape, dtype in scratch]
        + [pltpu.SemaphoreType.DMA((COPIES,)), pltpu.SemaphoreType.DMA((COPIES,))],
        compiler_params=pltpu.CompilerParams(
            collective_id=0, has_side_effects=True, vmem_limit_bytes=48 * 2**20
        ),
        name="block",
    )(
        slot_tile,
        land,
        features.reshape(512, 128),
        cotangent.reshape(512, 128),
        dw_kernel,
        dw_bias.reshape(1, 128),
        ln_gain.reshape(8, 128),
        ln_bias.reshape(8, 128),
        w_in,
        b_in.reshape(1, 512),
        w_out,
        b_out.reshape(1, 128),
        layer_scale.reshape(1, 128),
    )
    return output.reshape(features.shape), grad_in, grad_out.T


def solution(mesh):
    return jax.shard_map(
        body,
        mesh=mesh,
        in_specs=(
            P("space", None, None, "chan"),
            P(),
            P(),
            P(None, None, "chan"),
            P("chan"),
            P(),
            P(),
            P("space", "chan"),
            P("chan"),
            P("chan", "space"),
            P("chan"),
            P("chan"),
            P("space", None, None, "chan"),
        ),
        out_specs=(P("space", None, None, "chan"), P("space", "chan"), P("chan", "space")),
        check_vma=False,
    )
```

```python
import jax
import jax.numpy as jnp
from jax import lax
from jax.experimental import pallas as pl
from jax.experimental.pallas import tpu as pltpu
from jax.sharding import PartitionSpec as P

MESH = pl.DeviceIdType.MESH
F32, BF16 = jnp.float32, jnp.bfloat16
FAR = (1, 3, 2)
COPIES = 120


def wrap4(value):
    return lax.rem(value + 4, 4)


class Place:
    def __init__(self):
        self.space, self.chan = lax.axis_index("space"), lax.axis_index("chan")
        self.x, self.zh, self.core = self.space // 8, (self.space // 2) % 4, self.space % 2
        self.zl, self.y = self.chan // 4, self.chan % 4

    def slot(self, dx=0, dz=0, other=False):
        core = 1 - self.core if other else self.core
        return wrap4(self.x + dx) * 8 + wrap4(self.zh + dz) * 2 + core

    def part(self, dy=0, other=False):
        return (1 - self.zl if other else self.zl) * 4 + wrap4(self.y + dy)

    def ahead_x(self, d):
        return self.slot(dx=d), self.chan

    def ahead_z(self, d):
        return self.slot(dz=d), self.chan

    def ahead_y(self, d):
        return self.space, self.part(dy=d)

    def other_core(self):
        return self.slot(other=True), self.chan

    def other_zl(self):
        return self.space, self.part(other=True)

    def across(self, d):
        return self.slot(dx=d, other=True), self.chan

    def peers(self):
        ahead = (self.ahead_x, self.ahead_z, self.ahead_y, self.across)
        return [f(d) for f in ahead for d in FAR] + [self.other_core(), self.other_zl()]


class Links:
    def __init__(self, send_sems, recv_sems):
        self.send_sems, self.recv_sems, self.sent = send_sems, recv_sems, []

    def describe(self, number, source, target, device):
        return pltpu.make_async_remote_copy(
            src_ref=source,
            dst_ref=target,
            send_sem=self.send_sems.at[number],
            recv_sem=self.recv_sems.at[number],
            device_id=device,
            device_id_type=MESH,
        )

    def start(self, source, target, device):
        number = len(self.sent)
        assert number < COPIES
        copy = self.describe(number, source, target, device)
        copy.start()
        self.sent.append(copy)
        return number, device

    def landed(self, ticket, where):
        self.describe(ticket[0], where, where, ticket[1]).wait_recv()

    def finish(self):
        for copy in self.sent:
            copy.wait_send()


class SpaceGather:
    def __init__(self, links, place, block):
        self.links, self.place, self.block = links, place, block
        self.over_z, self.over_x, self.over_core = {}, {}, {}

    def send(self, block, device):
        return self.links.start(block, block, device)

    def own_z(self):
        place = self.place
        mine = self.block(place.slot())
        for d in FAR:
            self.over_z[d] = self.send(mine, (place.slot(dz=d), place.chan))

    def spread(self, d):
        place = self.place
        block = self.block(place.slot(dz=-d))
        if d:
            self.links.landed(self.over_z[d], block)
        for e in FAR:
            self.over_x[d, e] = self.send(block, (place.slot(dx=e), place.chan))
        self.over_core[d, 0] = self.send(block, (place.slot(other=True), place.chan))

    def cross(self, d, e):
        place = self.place
        block = self.block(place.slot(dx=-e, dz=-d))
        self.links.landed(self.over_x[d, e], block)
        self.over_core[d, e] = self.send(block, (place.slot(other=True), place.chan))

    def wait(self):
        place = self.place
        for (d, e), ticket in self.over_core.items():
            self.links.landed(ticket, self.block(place.slot(dx=-e, dz=-d, other=True)))


class ChanGather:
    def __init__(self, links, place, block):
        self.links, self.place, self.block = links, place, block
        self.over_y = {}

    def own_zl(self):
        mine = self.block(self.place.part())
        self.over_zl = self.links.start(mine, mine, self.place.other_zl())

    def own_y(self):
        self.spread(self.block(self.place.part()), False)

    def spread(self, block, other):
        place = self.place
        for d in FAR:
            self.over_y[d, other] = self.links.start(block, block, (place.space, place.part(dy=d)))

    def cross(self):
        block = self.block(self.place.part(other=True))
        self.links.landed(self.over_zl, block)
        self.spread(block, True)

    def wait(self):
        for (d, other), ticket in self.over_y.items():
            self.links.landed(ticket, self.block(self.place.part(dy=-d, other=other)))


class ChanGatherY(ChanGather):
    def cross(self):
        self.over_z = {}
        for d in FAR:
            block = self.block(self.place.part(dy=-d))
            self.links.landed(self.over_y[d, False], block)
            self.over_z[d] = self.links.start(block, block, self.place.other_zl())

    def wait(self):
        self.links.landed(self.over_zl, self.block(self.place.part(other=True)))
        for d in FAR:
            self.links.landed(self.over_z[d], self.block(self.place.part(dy=-d, other=True)))


class RingSum:
    def __init__(self, links, ahead, part, held):
        self.links, self.ahead, self.part, self.held = links, ahead, part, held
        self.tickets = {}

    def send(self, name, value, source, target, k):
        self.held[source] = value.astype(BF16)
        self.tickets[name] = self.links.start(
            self.held.at[source], self.held.at[target], self.ahead(k)
        )

    def take(self, name, where):
        self.links.landed(self.tickets[name], self.held.at[where])
        return self.held[where].astype(F32)

    def far(self):
        self.send("far0", self.part(2, 0), 0, 2, 1)
        self.send("far1", self.part(2, 1), 1, 3, 3)

    def near(self):
        self.send((0, 1), self.part(1, 1), 5, 9, 1)
        self.send((1, 0), self.part(3, 0), 6, 10, 3)

    def relay(self):
        self.send((0, 0), self.part(1, 0) + self.take("far0", 2), 4, 8, 1)
        self.send((1, 1), self.part(3, 1) + self.take("far1", 3), 7, 11, 3)

    def total(self, h):
        return self.part(0, h) + self.take((0, h), 8 + h) + self.take((1, h), 10 + h)


class DirectSum:
    def __init__(self, links, ahead, part, held):
        self.links, self.ahead, self.part, self.held = links, ahead, part, held
        self.tickets = {}

    def start(self):
        for k in FAR:
            self.held[k - 1] = self.part(k).astype(BF16)
            self.tickets[k] = self.links.start(
                self.held.at[k - 1], self.held.at[k + 2], self.ahead(k)
            )

    def total(self):
        total = self.part(0)
        for k in FAR:
            self.links.landed(self.tickets[k], self.held.at[k + 2])
            total = total + self.held[k + 2].astype(F32)
        return total


def kernel(
    slot_tile, land, feat_in, cot_in, dw_in, dw_bias_in, gain_in, shift_in, w_in, b_in_in, w_out_in,
    b_out_in, scale_in,
    out, gin, gout,
    feat, cot, dw, dw_bias, gain, shift, b_in, b_out, scale,
    xpad, cacc, hbuf, hsel, hsend, hrecv, hacc, wbuf, sbuf, dbuf0, dbuf1, nbuf, pre, qbuf, hid, back,
    gacc, gsend, gcore, gx, gown, gz, mx, mown, mzs, mzr,
    load_sems, send_sems, recv_sems,
):
    place, links = Place(), Links(send_sems, recv_sems)
    core, zl = place.core, place.zl
    first = place.space * 2
    barrier = pltpu.get_barrier_semaphore()
    for peer in place.peers():
        pl.semaphore_signal(barrier, inc=1, device_id=peer, device_id_type=MESH)
    loads = {}
    for name, source, target in (
        ("feat", feat_in, feat),
        ("scale", scale_in, scale),
        ("cot", cot_in, cot),
        ("w_in", w_in, wbuf.at[place.space, 0]),
        ("w_out", w_out_in, wbuf.at[place.space, 1]),
        ("dw", dw_in, dw),
        ("dw_bias", dw_bias_in, dw_bias),
        ("gain", gain_in, gain),
        ("shift", shift_in, shift),
        ("b_in", b_in_in, b_in),
        ("b_out", b_out_in, b_out),
    ):
        loads[name] = pltpu.make_async_copy(source, target, load_sems.at[len(loads)])
        loads[name].start()

    xpad[...] = jnp.zeros((2, 22, 32, 128), F32)
    hacc[...] = jnp.zeros((2, 2, 3, 32, 128), F32)
    tiles = [slot_tile[first + t] for t in range(2)]
    lands = [land[tile].astype(F32) for tile in tiles]
    loads["feat"].wait()
    for t in range(2):
        masked = feat[t * 256 : (t + 1) * 256, :].astype(F32) * lands[t]
        xpad[t, 3:19, 8:24, :] = masked.reshape(16, 16, 128)
        for side, begin in ((0, 0), (1, 13)):
            for q in range(3):
                column = xpad[t, 3:19, 8 + begin + q, :]
                hbuf[0, t * 2 + side, q] = column.astype(BF16)
    pl.semaphore_wait(barrier, len(place.peers()))

    dests = [(d, other) for other in (False, True) for d in range(4)]
    wanted = [
        [slot_tile[place.slot(dx=d, other=other) * 2 + t] for t in range(2)] for d, other in dests
    ]

    def pick(k):
        held = [slot_tile[place.slot(dz=-k) * 2 + i] for i in range(2)]
        strips = [hbuf[k, i].astype(F32) for i in range(4)]
        for n in range(8):
            for t in range(2):
                for side, step in ((0, -1), (1, 1)):
                    chosen = [(held[i] == wanted[n][t] + step).astype(F32) for i in range(2)]
                    found = strips[1 - side] * chosen[0] + strips[3 - side] * chosen[1]
                    if k:
                        found = found + hsel[n, t, side]
                    hsel[n, t, side] = found

    weights = SpaceGather(links, place, lambda s: wbuf.at[s])
    slopes = ChanGather(links, place, lambda c: sbuf.at[c])
    dbufs = (dbuf0, dbuf1)
    convs = [
        kind(links, place, lambda c, held=held: held.at[c])
        for kind, held in zip((ChanGather, ChanGatherY), dbufs)
    ]

    halo_z = {d: links.start(hbuf.at[0], hbuf.at[d], place.ahead_z(d)) for d in FAR}
    loads["scale"].wait()
    loads["cot"].wait()
    for t in range(2):
        rows = slice(t * 256, (t + 1) * 256)
        sbuf[place.chan, rows] = (cot[rows, :].astype(F32) * lands[t] * scale[...]).astype(BF16)
    slopes.own_y()
    slopes.own_zl()
    for name in ("w_in", "w_out"):
        loads[name].wait()
    weights.spread(0)
    pick(0)

    for name in ("dw", "dw_bias"):
        loads[name].wait()

    def inner(n, carry):
        t, i = n // 2, n % 2
        total = jnp.zeros((8, 16, 128), F32) + dw_bias[...][None]
        for e in range(7):
            rows = xpad[t, pl.ds(i * 8, 14), 5 + e : 21 + e, :]
            for a in range(7):
                total = total + dw[a, e : e + 1, :][None] * rows[a : a + 8]
        cacc[t, pl.ds(i * 8, 8)] = total
        return carry

    lax.fori_loop(0, 4, inner, 0)
    for d in FAR:
        links.landed(halo_z[d], hbuf.at[d])
        pick(d)
    halo_x = {}
    for n in (5, 7, 1, 3, 6, 2, 4):
        d, other = dests[n]
        hsend[n] = hsel[n].astype(BF16)
        device = place.across(d) if other else place.ahead_x(d)
        halo_x[n] = links.start(hsend.at[n], hrecv.at[n], device)
    slopes.cross()
    weights.own_z()
    for t in range(2):
        for side in range(2):
            hacc[t, side, :, 8:24] = hsel[0, t, side]
    for n, ticket in halo_x.items():
        links.landed(ticket, hrecv.at[n])
        for t in range(2):
            for side in range(2):
                hacc[t, side, :, 8:24] += hrecv[n, t, side].astype(F32)

    for t in range(2):
        for side in range(2):
            for q in range(3):
                total = jnp.zeros((16, 128), F32)
                for j in range(q, 3) if side == 0 else range(q + 1):
                    e = j - q if side == 0 else 6 + j - q
                    for a in range(7):
                        total = total + dw[a, e : e + 1, :] * hacc[t, side, j, 5 + a : 21 + a]
                cacc[t, :, 13 * side + q, :] += total
        dbufs[t][place.chan] = cacc[t].reshape(256, 128).astype(BF16)
        if t:
            convs[t].own_y()
            convs[t].own_zl()
        else:
            convs[t].own_zl()
            convs[t].own_y()

    for d in (1, 3):
        weights.spread(d)
    convs[0].cross()
    weights.spread(2)
    convs[1].cross()
    for d in (0,) + FAR:
        for e in FAR:
            weights.cross(d, e)
    slopes.wait()
    weights.wait()
    for name in ("gain", "shift", "b_in", "b_out"):
        loads[name].wait()

    for t in range(2):
        rows = slice(t * 256, (t + 1) * 256)
        slope_rows = jnp.concatenate([sbuf[c, rows] for c in range(8)], axis=1)
        qbuf[rows] = jnp.dot(
            slope_rows, wbuf[:, 1].reshape(1024, 512), preferred_element_type=F32
        )

    for t in range(2):
        convs[t].wait()

        def norm(i, carry):
            at = pl.ds(pl.multiple_of(i * 64, 64), 64)
            x = dbufs[t][:, at, :].astype(F32)
            mean = jnp.sum(jnp.sum(x, axis=0), axis=1, keepdims=True) * (1.0 / 1024)
            x = x - mean[None]
            spread = jnp.sum(jnp.sum(x * x, axis=0), axis=1, keepdims=True) * (1.0 / 1024)
            x = x * lax.rsqrt(spread + 1e-06)[None]
            to = pl.ds(pl.multiple_of(t * 256 + i * 64, 64), 64)
            for c in range(8):
                y = x[c] * gain[c : c + 1] + shift[c : c + 1]
                nbuf[to, c * 128 : (c + 1) * 128] = y.astype(BF16)
            return carry

        lax.fori_loop(0, 4, norm, 0)
        rows = slice(t * 256, (t + 1) * 256)
        pre[...] = (
            jnp.dot(nbuf[rows], wbuf[:, 0].reshape(1024, 512), preferred_element_type=F32)
            + b_in[...]
        )

        def act(i, carry):
            at = pl.ds(pl.multiple_of(i * 32, 32), 32)
            to = pl.ds(pl.multiple_of(t * 256 + i * 32, 32), 32)
            p = pre[at]
            below = 0.5 * (1.0 + lax.erf(p * 0.7071067811865476))
            hid[to] = (p * below).astype(BF16)
            rise = below + p * jnp.exp(-0.5 * p * p) * 0.3989422804014327
            back[to] = (qbuf[to] * rise).astype(BF16)
            return carry

        lax.fori_loop(0, 8, act, 0)

    over_core = {}
    for g in (1, 0):
        for i in range(4):
            if g:
                left = jnp.concatenate((sbuf[2 * i], sbuf[2 * i + 1]), axis=1)
            else:
                left = nbuf[:, i * 256 : (i + 1) * 256]
            summed = lax.dot_general(
                left, (hid if g else back)[...], (((0,), (0,)), ((), ())),
                preferred_element_type=F32,
            )
            gacc[g, 4 * i : 4 * i + 4] = summed.reshape(4, 2, 32, 512)
            gsend[g, 4 * i : 4 * i + 4] = gacc[g, 4 * i : 4 * i + 4, 1 - core].astype(BF16)
        over_core[g] = links.start(gsend.at[g], gcore.at[g], place.other_core())

    def grad_part(g):
        def part(k, h):
            at = pl.ds(wrap4(place.x + k) * 4 + 2 * h, 2)
            return gacc[g, at, core] + gcore[g, at].astype(F32)

        return part

    over_x = [RingSum(links, place.ahead_x, grad_part(g), gx.at[g]) for g in range(2)]
    over_z = [
        DirectSum(
            links, place.ahead_z, lambda k, g=g: gown[g, wrap4(place.zh + k)], gz.at[g]
        )
        for g in range(2)
    ]
    for g in (1, 0):
        links.landed(over_core[g], gcore.at[g])
        over_x[g].far()
        if g:
            over_x[g].near()

    for k in (2, 1, 3, 0):
        to = wrap4(place.y + k)
        columns = jnp.concatenate(
            [wbuf[pl.ds(i * 16 + to * 4, 4), 1].reshape(128, 512) for i in range(2)], axis=0
        )
        partial = lax.dot_general(
            hid[...], columns, (((1,), (1,)), ((), ())), preferred_element_type=F32
        )
        for t in range(2):
            for i in range(2):
                mown[k, t, i] = partial[t * 256 : (t + 1) * 256, i * 128 : (i + 1) * 128]
    over_y = RingSum(links, place.ahead_y, lambda k, h: mown[k, h], mx)
    over_y.far()
    over_y.near()
    over_x[1].relay()
    over_x[0].near()
    over_x[0].relay()
    over_y.relay()
    for g in (1, 0):
        for h in range(2):
            gown[g, 2 * h : 2 * h + 2] = over_x[g].total(h)
        over_z[g].start()
    for t in range(2):
        mown[0, t] = over_y.total(t)
        mzs[t] = mown[0, t, 1 - zl].astype(BF16)
    mixed_z = links.start(mzs, mzr, place.other_zl())
    links.landed(mixed_z, mzr)
    for t in range(2):
        rows = slice(t * 256, (t + 1) * 256)
        mixed = mown[0, t, zl] + mzr[t].astype(F32)
        value = feat[rows, :].astype(F32) + scale[...] * (mixed + b_out[...])
        out[rows, :] = (lands[t] * value).astype(BF16)
    for g, result in ((1, gout), (0, gin)):
        result[...] = over_z[g].total()
    links.finish()


def body(
    features, slot_tile, land, dw_kernel, dw_bias, ln_gain, ln_bias, w_in, b_in, w_out, b_out,
    layer_scale, cotangent,
):
    vmem = pl.BlockSpec(memory_space=pltpu.VMEM)
    smem = pl.BlockSpec(memory_space=pltpu.SMEM)
    scratch = [
        ((512, 128), BF16),
        ((512, 128), BF16),
        ((7, 7, 128), F32),
        ((1, 128), F32),
        ((8, 128), F32),
        ((8, 128), F32),
        ((1, 512), F32),
        ((1, 128), F32),
        ((1, 128), F32),
        ((2, 22, 32, 128), F32),
        ((2, 16, 16, 128), F32),
        ((4, 4, 3, 16, 128), BF16),
        ((8, 2, 2, 3, 16, 128), F32),
        ((8, 2, 2, 3, 16, 128), BF16),
        ((8, 2, 2, 3, 16, 128), BF16),
        ((2, 2, 3, 32, 128), F32),
        ((32, 2, 32, 512), BF16),
        ((8, 512, 128), BF16),
        ((8, 256, 128), BF16),
        ((8, 256, 128), BF16),
        ((512, 1024), BF16),
        ((256, 512), F32),
        ((512, 512), F32),
        ((512, 512), BF16),
        ((512, 512), BF16),
        ((2, 16, 2, 32, 512), F32),
        ((2, 16, 32, 512), BF16),
        ((2, 16, 32, 512), BF16),
        ((2, 12, 2, 32, 512), BF16),
        ((2, 4, 32, 512), F32),
        ((2, 6, 32, 512), BF16),
        ((12, 2, 256, 128), BF16),
        ((4, 2, 2, 256, 128), F32),
        ((2, 256, 128), BF16),
        ((2, 256, 128), BF16),
    ]
    output, grad_in, grad_out = pl.pallas_call(
        kernel,
        out_shape=(
            jax.ShapeDtypeStruct((512, 128), BF16),
            jax.ShapeDtypeStruct((32, 512), F32),
            jax.ShapeDtypeStruct((32, 512), F32),
        ),
        in_specs=[smem, smem] + [pl.BlockSpec(memory_space=pltpu.HBM)] * 11,
        out_specs=(vmem, vmem, vmem),
        scratch_shapes=[pltpu.VMEM(shape, dtype) for shape, dtype in scratch]
        + [pltpu.SemaphoreType.DMA((11,)), pltpu.SemaphoreType.DMA((COPIES,)), pltpu.SemaphoreType.DMA((COPIES,))],
        compiler_params=pltpu.CompilerParams(
            collective_id=0, has_side_effects=True, vmem_limit_bytes=60 * 2**20
        ),
        name="block",
    )(
        slot_tile,
        land,
        features.reshape(512, 128),
        cotangent.reshape(512, 128),
        dw_kernel,
        dw_bias.reshape(1, 128),
        ln_gain.reshape(8, 128),
        ln_bias.reshape(8, 128),
        w_in,
        b_in.reshape(1, 512),
        w_out.T,
        b_out.reshape(1, 128),
        layer_scale.reshape(1, 128),
    )
    return output.reshape(features.shape), grad_in, grad_out.T


def solution(mesh):
    return jax.shard_map(
        body,
        mesh=mesh,
        in_specs=(
            P("space", None, None, "chan"),
            P(),
            P(),
            P(None, None, "chan"),
            P("chan"),
            P(),
            P(),
            P("space", "chan"),
            P("chan"),
            P("chan", "space"),
            P("chan"),
            P("chan"),
            P("space", None, None, "chan"),
        ),
        out_specs=(P("space", None, None, "chan"), P("space", "chan"), P("chan", "space")),
        check_vma=False,
    )
```

```python
import jax
import jax.numpy as jnp
from jax import lax
from jax.experimental import pallas as pl
from jax.experimental.pallas import tpu as pltpu
from jax.sharding import PartitionSpec as P

MESH = pl.DeviceIdType.MESH
F32, BF16 = jnp.float32, jnp.bfloat16
FAR = (1, 3, 2)
COPIES = 120


def wrap4(value):
    return lax.rem(value + 4, 4)


class Place:
    def __init__(self):
        self.space, self.chan = lax.axis_index("space"), lax.axis_index("chan")
        self.x, self.zh, self.core = self.space // 8, (self.space // 2) % 4, self.space % 2
        self.zl, self.y = self.chan // 4, self.chan % 4

    def slot(self, dx=0, dz=0, other=False):
        core = 1 - self.core if other else self.core
        return wrap4(self.x + dx) * 8 + wrap4(self.zh + dz) * 2 + core

    def part(self, dy=0, other=False):
        return (1 - self.zl if other else self.zl) * 4 + wrap4(self.y + dy)

    def ahead_x(self, d):
        return self.slot(dx=d), self.chan

    def ahead_z(self, d):
        return self.slot(dz=d), self.chan

    def ahead_y(self, d):
        return self.space, self.part(dy=d)

    def other_core(self):
        return self.slot(other=True), self.chan

    def other_zl(self):
        return self.space, self.part(other=True)

    def across(self, d):
        return self.slot(dx=d, other=True), self.chan

    def peers(self):
        ahead = (self.ahead_x, self.ahead_z, self.ahead_y, self.across)
        return [f(d) for f in ahead for d in FAR] + [self.other_core(), self.other_zl()]


class Links:
    def __init__(self, send_sems, recv_sems):
        self.send_sems, self.recv_sems, self.sent = send_sems, recv_sems, []

    def describe(self, number, source, target, device):
        return pltpu.make_async_remote_copy(
            src_ref=source,
            dst_ref=target,
            send_sem=self.send_sems.at[number],
            recv_sem=self.recv_sems.at[number],
            device_id=device,
            device_id_type=MESH,
        )

    def start(self, source, target, device):
        number = len(self.sent)
        assert number < COPIES
        copy = self.describe(number, source, target, device)
        copy.start()
        self.sent.append(copy)
        return number, device

    def landed(self, ticket, where):
        self.describe(ticket[0], where, where, ticket[1]).wait_recv()

    def finish(self):
        for copy in self.sent:
            copy.wait_send()


class SpaceGather:
    def __init__(self, links, place, block):
        self.links, self.place, self.block = links, place, block
        self.over_z, self.over_x, self.over_core = {}, {}, {}

    def send(self, block, device):
        return self.links.start(block, block, device)

    def own_z(self):
        place = self.place
        mine = self.block(place.slot())
        for d in FAR:
            self.over_z[d] = self.send(mine, (place.slot(dz=d), place.chan))

    def spread(self, d):
        place = self.place
        block = self.block(place.slot(dz=-d))
        if d:
            self.links.landed(self.over_z[d], block)
        for e in FAR:
            self.over_x[d, e] = self.send(block, (place.slot(dx=e), place.chan))
        self.over_core[d, 0] = self.send(block, (place.slot(other=True), place.chan))

    def cross(self, d, e):
        place = self.place
        block = self.block(place.slot(dx=-e, dz=-d))
        self.links.landed(self.over_x[d, e], block)
        self.over_core[d, e] = self.send(block, (place.slot(other=True), place.chan))

    def wait(self):
        place = self.place
        for (d, e), ticket in self.over_core.items():
            self.links.landed(ticket, self.block(place.slot(dx=-e, dz=-d, other=True)))


class ChanGather:
    def __init__(self, links, place, block):
        self.links, self.place, self.block = links, place, block
        self.over_y = {}

    def own_zl(self):
        mine = self.block(self.place.part())
        self.over_zl = self.links.start(mine, mine, self.place.other_zl())

    def own_y(self):
        self.spread(self.block(self.place.part()), False)

    def spread(self, block, other):
        place = self.place
        for d in FAR:
            self.over_y[d, other] = self.links.start(block, block, (place.space, place.part(dy=d)))

    def cross(self):
        block = self.block(self.place.part(other=True))
        self.links.landed(self.over_zl, block)
        self.spread(block, True)

    def wait(self):
        for (d, other), ticket in self.over_y.items():
            self.links.landed(ticket, self.block(self.place.part(dy=-d, other=other)))


class ChanGatherY(ChanGather):
    def cross(self):
        self.over_z = {}
        for d in FAR:
            block = self.block(self.place.part(dy=-d))
            self.links.landed(self.over_y[d, False], block)
            self.over_z[d] = self.links.start(block, block, self.place.other_zl())

    def wait(self):
        self.links.landed(self.over_zl, self.block(self.place.part(other=True)))
        for d in FAR:
            self.links.landed(self.over_z[d], self.block(self.place.part(dy=-d, other=True)))


class RingSum:
    def __init__(self, links, ahead, part, held):
        self.links, self.ahead, self.part, self.held = links, ahead, part, held
        self.tickets = {}

    def send(self, name, value, source, target, k):
        self.held[source] = value.astype(BF16)
        self.tickets[name] = self.links.start(
            self.held.at[source], self.held.at[target], self.ahead(k)
        )

    def take(self, name, where):
        self.links.landed(self.tickets[name], self.held.at[where])
        return self.held[where].astype(F32)

    def far(self):
        self.send("far0", self.part(2, 0), 0, 2, 1)
        self.send("far1", self.part(2, 1), 1, 3, 3)

    def near(self):
        self.send((0, 1), self.part(1, 1), 5, 9, 1)
        self.send((1, 0), self.part(3, 0), 6, 10, 3)

    def relay(self):
        self.send((0, 0), self.part(1, 0) + self.take("far0", 2), 4, 8, 1)
        self.send((1, 1), self.part(3, 1) + self.take("far1", 3), 7, 11, 3)

    def total(self, h):
        return self.part(0, h) + self.take((0, h), 8 + h) + self.take((1, h), 10 + h)


class DirectSum:
    def __init__(self, links, ahead, part, held):
        self.links, self.ahead, self.part, self.held = links, ahead, part, held
        self.tickets = {}

    def start(self):
        for k in FAR:
            self.held[k - 1] = self.part(k).astype(BF16)
            self.tickets[k] = self.links.start(
                self.held.at[k - 1], self.held.at[k + 2], self.ahead(k)
            )

    def total(self):
        total = self.part(0)
        for k in FAR:
            self.links.landed(self.tickets[k], self.held.at[k + 2])
            total = total + self.held[k + 2].astype(F32)
        return total


def kernel(
    slot_tile, land, feat_in, cot_in, dw_in, dw_bias_in, gain_in, shift_in, w_in, b_in_in, w_out_in,
    b_out_in, scale_in,
    out, gin, gout,
    feat, cot, dw, dw_bias, gain, shift, b_in, b_out, scale,
    xpad, cacc, hbuf, hsel, hsend, hrecv, hacc, wbuf, sbuf, dbuf0, dbuf1, nbuf, pre, qbuf, hid, back,
    gacc, gsend, gcore, gx, gown, gz, mx, mown, mzs, mzr,
    load_sems, send_sems, recv_sems,
):
    place, links = Place(), Links(send_sems, recv_sems)
    core, zl = place.core, place.zl
    first = place.space * 2
    barrier = pltpu.get_barrier_semaphore()
    for peer in place.peers():
        pl.semaphore_signal(barrier, inc=1, device_id=peer, device_id_type=MESH)
    loads = {}
    for name, source, target in (
        ("feat", feat_in, feat),
        ("scale", scale_in, scale),
        ("cot", cot_in, cot),
        ("w_in", w_in, wbuf.at[place.space, 0]),
        ("w_out", w_out_in, wbuf.at[place.space, 1]),
        ("dw", dw_in, dw),
        ("dw_bias", dw_bias_in, dw_bias),
        ("gain", gain_in, gain),
        ("shift", shift_in, shift),
        ("b_in", b_in_in, b_in),
        ("b_out", b_out_in, b_out),
    ):
        loads[name] = pltpu.make_async_copy(source, target, load_sems.at[len(loads)])
        loads[name].start()

    xpad[...] = jnp.zeros((2, 22, 32, 128), F32)
    hacc[...] = jnp.zeros((2, 2, 3, 32, 128), F32)
    tiles = [slot_tile[first + t] for t in range(2)]
    lands = [land[tile].astype(F32) for tile in tiles]
    loads["feat"].wait()
    for t in range(2):
        masked = feat[t * 256 : (t + 1) * 256, :].astype(F32) * lands[t]
        xpad[t, 3:19, 8:24, :] = masked.reshape(16, 16, 128)
        for side, begin in ((0, 0), (1, 13)):
            for q in range(3):
                column = xpad[t, 3:19, 8 + begin + q, :]
                hbuf[0, t * 2 + side, q] = column.astype(BF16)
    pl.semaphore_wait(barrier, len(place.peers()))

    dests = [(d, other) for other in (False, True) for d in range(4)]
    wanted = [
        [slot_tile[place.slot(dx=d, other=other) * 2 + t] for t in range(2)] for d, other in dests
    ]

    def pick(k):
        held = [slot_tile[place.slot(dz=-k) * 2 + i] for i in range(2)]
        strips = [hbuf[k, i].astype(F32) for i in range(4)]
        for n in range(8):
            for t in range(2):
                for side, step in ((0, -1), (1, 1)):
                    chosen = [(held[i] == wanted[n][t] + step).astype(F32) for i in range(2)]
                    found = strips[1 - side] * chosen[0] + strips[3 - side] * chosen[1]
                    if k:
                        found = found + hsel[n, t, side]
                    hsel[n, t, side] = found

    weights = SpaceGather(links, place, lambda s: wbuf.at[s])
    slopes = ChanGather(links, place, lambda c: sbuf.at[c])
    dbufs = (dbuf0, dbuf1)
    convs = [
        kind(links, place, lambda c, held=held: held.at[c])
        for kind, held in zip((ChanGather, ChanGatherY), dbufs)
    ]

    halo_z = {d: links.start(hbuf.at[0], hbuf.at[d], place.ahead_z(d)) for d in FAR}
    loads["scale"].wait()
    loads["cot"].wait()
    for t in range(2):
        rows = slice(t * 256, (t + 1) * 256)
        sbuf[place.chan, rows] = (cot[rows, :].astype(F32) * lands[t] * scale[...]).astype(BF16)
    slopes.own_y()
    slopes.own_zl()
    for name in ("w_in", "w_out"):
        loads[name].wait()
    weights.spread(0)
    pick(0)

    for name in ("dw", "dw_bias"):
        loads[name].wait()

    def inner(n, carry):
        t, i = n // 2, n % 2
        total = jnp.zeros((8, 16, 128), F32) + dw_bias[...][None]
        for e in range(7):
            rows = xpad[t, pl.ds(i * 8, 14), 5 + e : 21 + e, :]
            for a in range(7):
                total = total + dw[a, e : e + 1, :][None] * rows[a : a + 8]
        cacc[t, pl.ds(i * 8, 8)] = total
        return carry

    lax.fori_loop(0, 4, inner, 0)
    for d in FAR:
        links.landed(halo_z[d], hbuf.at[d])
        pick(d)
    halo_x = {}
    for n in (5, 7, 1, 3, 6, 2, 4):
        d, other = dests[n]
        hsend[n] = hsel[n].astype(BF16)
        device = place.across(d) if other else place.ahead_x(d)
        halo_x[n] = links.start(hsend.at[n], hrecv.at[n], device)
    slopes.cross()
    weights.own_z()
    for t in range(2):
        for side in range(2):
            hacc[t, side, :, 8:24] = hsel[0, t, side]
    for n, ticket in halo_x.items():
        links.landed(ticket, hrecv.at[n])
        for t in range(2):
            for side in range(2):
                hacc[t, side, :, 8:24] += hrecv[n, t, side].astype(F32)

    for t in range(2):
        for side in range(2):
            for q in range(3):
                total = jnp.zeros((16, 128), F32)
                for j in range(q, 3) if side == 0 else range(q + 1):
                    e = j - q if side == 0 else 6 + j - q
                    for a in range(7):
                        total = total + dw[a, e : e + 1, :] * hacc[t, side, j, 5 + a : 21 + a]
                cacc[t, :, 13 * side + q, :] += total
        dbufs[t][place.chan] = cacc[t].reshape(256, 128).astype(BF16)
        if t:
            convs[t].own_y()
            convs[t].own_zl()
        else:
            convs[t].own_zl()
            convs[t].own_y()

    for d in (1, 3):
        weights.spread(d)
    convs[0].cross()
    weights.spread(2)
    convs[1].cross()
    for d in (0,) + FAR:
        for e in FAR:
            weights.cross(d, e)
    slopes.wait()
    weights.wait()
    for name in ("gain", "shift", "b_in", "b_out"):
        loads[name].wait()

    for t in range(2):
        rows = slice(t * 256, (t + 1) * 256)
        slope_rows = jnp.concatenate([sbuf[c, rows] for c in range(8)], axis=1)
        qbuf[rows] = jnp.dot(
            slope_rows, wbuf[:, 1].reshape(1024, 512), preferred_element_type=F32
        )

    for t in range(2):
        convs[t].wait()

        def norm(i, carry):
            at = pl.ds(pl.multiple_of(i * 64, 64), 64)
            x = dbufs[t][:, at, :].astype(F32)
            mean = jnp.sum(jnp.sum(x, axis=0), axis=1, keepdims=True) * (1.0 / 1024)
            x = x - mean[None]
            spread = jnp.sum(jnp.sum(x * x, axis=0), axis=1, keepdims=True) * (1.0 / 1024)
            x = x * lax.rsqrt(spread + 1e-06)[None]
            to = pl.ds(pl.multiple_of(t * 256 + i * 64, 64), 64)
            for c in range(8):
                y = x[c] * gain[c : c + 1] + shift[c : c + 1]
                nbuf[to, c * 128 : (c + 1) * 128] = y.astype(BF16)
            return carry

        lax.fori_loop(0, 4, norm, 0)
        rows = slice(t * 256, (t + 1) * 256)
        pre[...] = (
            jnp.dot(nbuf[rows], wbuf[:, 0].reshape(1024, 512), preferred_element_type=F32)
            + b_in[...]
        )

        def act(i, carry):
            at = pl.ds(pl.multiple_of(i * 32, 32), 32)
            to = pl.ds(pl.multiple_of(t * 256 + i * 32, 32), 32)
            p = pre[at]
            below = 0.5 * (1.0 + lax.erf(p * 0.7071067811865476))
            hid[to] = (p * below).astype(BF16)
            rise = below + p * jnp.exp(-0.5 * p * p) * 0.3989422804014327
            back[to] = (qbuf[to] * rise).astype(BF16)
            return carry

        lax.fori_loop(0, 8, act, 0)

    over_core = {}
    for g in (1, 0):
        for i in range(4):
            if g:
                left = jnp.concatenate((sbuf[2 * i], sbuf[2 * i + 1]), axis=1)
            else:
                left = nbuf[:, i * 256 : (i + 1) * 256]
            summed = lax.dot_general(
                left, (hid if g else back)[...], (((0,), (0,)), ((), ())),
                preferred_element_type=F32,
            )
            gacc[g, 4 * i : 4 * i + 4] = summed.reshape(4, 2, 32, 512)
            gsend[g, 4 * i : 4 * i + 4] = gacc[g, 4 * i : 4 * i + 4, 1 - core].astype(BF16)
        over_core[g] = links.start(gsend.at[g], gcore.at[g], place.other_core())

    def grad_part(g):
        def part(k, h):
            at = pl.ds(wrap4(place.x + k) * 4 + 2 * h, 2)
            return gacc[g, at, core] + gcore[g, at].astype(F32)

        return part

    over_x = [RingSum(links, place.ahead_x, grad_part(g), gx.at[g]) for g in range(2)]
    over_z = [
        DirectSum(
            links, place.ahead_z, lambda k, g=g: gown[g, wrap4(place.zh + k)], gz.at[g]
        )
        for g in range(2)
    ]
    for g in (1, 0):
        links.landed(over_core[g], gcore.at[g])
        over_x[g].far()
        if g:
            over_x[g].near()

    for k in (2, 1, 3, 0):
        to = wrap4(place.y + k)
        columns = jnp.concatenate(
            [wbuf[pl.ds(i * 16 + to * 4, 4), 1].reshape(128, 512) for i in range(2)], axis=0
        )
        partial = lax.dot_general(
            hid[...], columns, (((1,), (1,)), ((), ())), preferred_element_type=F32
        )
        for t in range(2):
            for i in range(2):
                mown[k, t, i] = partial[t * 256 : (t + 1) * 256, i * 128 : (i + 1) * 128]
    over_y = RingSum(links, place.ahead_y, lambda k, h: mown[k, h], mx)
    over_y.far()
    over_y.near()
    over_x[1].relay()
    over_x[0].near()
    over_x[0].relay()
    for g in (1, 0):
        for h in range(2):
            gown[g, 2 * h : 2 * h + 2] = over_x[g].total(h)
        over_z[g].start()
        if g:
            over_y.relay()
    for t in range(2):
        mown[0, t] = over_y.total(t)
        mzs[t] = mown[0, t, 1 - zl].astype(BF16)
    mixed_z = links.start(mzs, mzr, place.other_zl())
    links.landed(mixed_z, mzr)
    for t in range(2):
        rows = slice(t * 256, (t + 1) * 256)
        mixed = mown[0, t, zl] + mzr[t].astype(F32)
        value = feat[rows, :].astype(F32) + scale[...] * (mixed + b_out[...])
        out[rows, :] = (lands[t] * value).astype(BF16)
    for g, result in ((1, gout), (0, gin)):
        result[...] = over_z[g].total()
    links.finish()


def body(
    features, slot_tile, land, dw_kernel, dw_bias, ln_gain, ln_bias, w_in, b_in, w_out, b_out,
    layer_scale, cotangent,
):
    vmem = pl.BlockSpec(memory_space=pltpu.VMEM)
    smem = pl.BlockSpec(memory_space=pltpu.SMEM)
    scratch = [
        ((512, 128), BF16),
        ((512, 128), BF16),
        ((7, 7, 128), F32),
        ((1, 128), F32),
        ((8, 128), F32),
        ((8, 128), F32),
        ((1, 512), F32),
        ((1, 128), F32),
        ((1, 128), F32),
        ((2, 22, 32, 128), F32),
        ((2, 16, 16, 128), F32),
        ((4, 4, 3, 16, 128), BF16),
        ((8, 2, 2, 3, 16, 128), F32),
        ((8, 2, 2, 3, 16, 128), BF16),
        ((8, 2, 2, 3, 16, 128), BF16),
        ((2, 2, 3, 32, 128), F32),
        ((32, 2, 32, 512), BF16),
        ((8, 512, 128), BF16),
        ((8, 256, 128), BF16),
        ((8, 256, 128), BF16),
        ((512, 1024), BF16),
        ((256, 512), F32),
        ((512, 512), F32),
        ((512, 512), BF16),
        ((512, 512), BF16),
        ((2, 16, 2, 32, 512), F32),
        ((2, 16, 32, 512), BF16),
        ((2, 16, 32, 512), BF16),
        ((2, 12, 2, 32, 512), BF16),
        ((2, 4, 32, 512), F32),
        ((2, 6, 32, 512), BF16),
        ((12, 2, 256, 128), BF16),
        ((4, 2, 2, 256, 128), F32),
        ((2, 256, 128), BF16),
        ((2, 256, 128), BF16),
    ]
    output, grad_in, grad_out = pl.pallas_call(
        kernel,
        out_shape=(
            jax.ShapeDtypeStruct((512, 128), BF16),
            jax.ShapeDtypeStruct((32, 512), F32),
            jax.ShapeDtypeStruct((32, 512), F32),
        ),
        in_specs=[smem, smem] + [pl.BlockSpec(memory_space=pltpu.HBM)] * 11,
        out_specs=(vmem, vmem, vmem),
        scratch_shapes=[pltpu.VMEM(shape, dtype) for shape, dtype in scratch]
        + [pltpu.SemaphoreType.DMA((11,)), pltpu.SemaphoreType.DMA((COPIES,)), pltpu.SemaphoreType.DMA((COPIES,))],
        compiler_params=pltpu.CompilerParams(
            collective_id=0, has_side_effects=True, vmem_limit_bytes=60 * 2**20
        ),
        name="block",
    )(
        slot_tile,
        land,
        features.reshape(512, 128),
        cotangent.reshape(512, 128),
        dw_kernel,
        dw_bias.reshape(1, 128),
        ln_gain.reshape(8, 128),
        ln_bias.reshape(8, 128),
        w_in,
        b_in.reshape(1, 512),
        w_out.T,
        b_out.reshape(1, 128),
        layer_scale.reshape(1, 128),
    )
    return output.reshape(features.shape), grad_in, grad_out.T


def solution(mesh):
    return jax.shard_map(
        body,
        mesh=mesh,
        in_specs=(
            P("space", None, None, "chan"),
            P(),
            P(),
            P(None, None, "chan"),
            P("chan"),
            P(),
            P(),
            P("space", "chan"),
            P("chan"),
            P("chan", "space"),
            P("chan"),
            P("chan"),
            P("space", None, None, "chan"),
        ),
        out_specs=(P("space", None, None, "chan"), P("space", "chan"), P("chan", "space")),
        check_vma=False,
    )
```

```python
import jax
import jax.numpy as jnp
from jax import lax
from jax.experimental import pallas as pl
from jax.experimental.pallas import tpu as pltpu
from jax.sharding import PartitionSpec as P

MESH = pl.DeviceIdType.MESH
F32, BF16 = jnp.float32, jnp.bfloat16
FAR = (1, 3, 2)
COPIES = 120


def wrap4(value):
    return lax.rem(value + 4, 4)


class Place:
    def __init__(self):
        self.space, self.chan = lax.axis_index("space"), lax.axis_index("chan")
        self.x, self.zh, self.core = self.space // 8, (self.space // 2) % 4, self.space % 2
        self.zl, self.y = self.chan // 4, self.chan % 4

    def slot(self, dx=0, dz=0, other=False):
        core = 1 - self.core if other else self.core
        return wrap4(self.x + dx) * 8 + wrap4(self.zh + dz) * 2 + core

    def part(self, dy=0, other=False):
        return (1 - self.zl if other else self.zl) * 4 + wrap4(self.y + dy)

    def ahead_x(self, d):
        return self.slot(dx=d), self.chan

    def ahead_z(self, d):
        return self.slot(dz=d), self.chan

    def ahead_y(self, d):
        return self.space, self.part(dy=d)

    def other_core(self):
        return self.slot(other=True), self.chan

    def other_zl(self):
        return self.space, self.part(other=True)

    def across(self, d):
        return self.slot(dx=d, other=True), self.chan

    def peers(self):
        ahead = (self.ahead_x, self.ahead_z, self.ahead_y, self.across)
        return [f(d) for f in ahead for d in FAR] + [self.other_core(), self.other_zl()]


class Links:
    def __init__(self, send_sems, recv_sems):
        self.send_sems, self.recv_sems, self.sent = send_sems, recv_sems, []

    def describe(self, number, source, target, device):
        return pltpu.make_async_remote_copy(
            src_ref=source,
            dst_ref=target,
            send_sem=self.send_sems.at[number],
            recv_sem=self.recv_sems.at[number],
            device_id=device,
            device_id_type=MESH,
        )

    def start(self, source, target, device):
        number = len(self.sent)
        assert number < COPIES
        copy = self.describe(number, source, target, device)
        copy.start()
        self.sent.append(copy)
        return number, device

    def landed(self, ticket, where):
        self.describe(ticket[0], where, where, ticket[1]).wait_recv()

    def finish(self):
        for copy in self.sent:
            copy.wait_send()


class SpaceGather:
    def __init__(self, links, place, block):
        self.links, self.place, self.block = links, place, block
        self.over_z, self.over_x, self.over_core = {}, {}, {}

    def send(self, block, device):
        return self.links.start(block, block, device)

    def own_z(self):
        place = self.place
        mine = self.block(place.slot())
        for d in FAR:
            self.over_z[d] = self.send(mine, (place.slot(dz=d), place.chan))

    def spread(self, d):
        place = self.place
        block = self.block(place.slot(dz=-d))
        if d:
            self.links.landed(self.over_z[d], block)
        for e in FAR:
            self.over_x[d, e] = self.send(block, (place.slot(dx=e), place.chan))
        self.over_core[d, 0] = self.send(block, (place.slot(other=True), place.chan))

    def cross(self, d, e):
        place = self.place
        block = self.block(place.slot(dx=-e, dz=-d))
        self.links.landed(self.over_x[d, e], block)
        self.over_core[d, e] = self.send(block, (place.slot(other=True), place.chan))

    def wait(self):
        place = self.place
        for (d, e), ticket in self.over_core.items():
            self.links.landed(ticket, self.block(place.slot(dx=-e, dz=-d, other=True)))


class ChanGather:
    def __init__(self, links, place, block):
        self.links, self.place, self.block = links, place, block
        self.over_y = {}

    def own_zl(self):
        mine = self.block(self.place.part())
        self.over_zl = self.links.start(mine, mine, self.place.other_zl())

    def own_y(self):
        self.spread(self.block(self.place.part()), False)

    def spread(self, block, other):
        place = self.place
        for d in FAR:
            self.over_y[d, other] = self.links.start(block, block, (place.space, place.part(dy=d)))

    def cross(self):
        block = self.block(self.place.part(other=True))
        self.links.landed(self.over_zl, block)
        self.spread(block, True)

    def wait(self):
        for (d, other), ticket in self.over_y.items():
            self.links.landed(ticket, self.block(self.place.part(dy=-d, other=other)))


class ChanGatherY(ChanGather):
    def cross(self):
        self.over_z = {}
        for d in FAR:
            block = self.block(self.place.part(dy=-d))
            self.links.landed(self.over_y[d, False], block)
            self.over_z[d] = self.links.start(block, block, self.place.other_zl())

    def wait(self):
        self.links.landed(self.over_zl, self.block(self.place.part(other=True)))
        for d in FAR:
            self.links.landed(self.over_z[d], self.block(self.place.part(dy=-d, other=True)))


class RingSum:
    def __init__(self, links, ahead, part, held):
        self.links, self.ahead, self.part, self.held = links, ahead, part, held
        self.tickets = {}

    def send(self, name, value, source, target, k):
        self.held[source] = value.astype(BF16)
        self.tickets[name] = self.links.start(
            self.held.at[source], self.held.at[target], self.ahead(k)
        )

    def take(self, name, where):
        self.links.landed(self.tickets[name], self.held.at[where])
        return self.held[where].astype(F32)

    def far(self):
        self.send("far0", self.part(2, 0), 0, 2, 1)
        self.send("far1", self.part(2, 1), 1, 3, 3)

    def near(self):
        self.send((0, 1), self.part(1, 1), 5, 9, 1)
        self.send((1, 0), self.part(3, 0), 6, 10, 3)

    def relay(self):
        self.send((0, 0), self.part(1, 0) + self.take("far0", 2), 4, 8, 1)
        self.send((1, 1), self.part(3, 1) + self.take("far1", 3), 7, 11, 3)

    def total(self, h):
        return self.part(0, h) + self.take((0, h), 8 + h) + self.take((1, h), 10 + h)


class DirectSum:
    def __init__(self, links, ahead, part, held):
        self.links, self.ahead, self.part, self.held = links, ahead, part, held
        self.tickets = {}

    def start(self):
        for k in FAR:
            self.held[k - 1] = self.part(k).astype(BF16)
            self.tickets[k] = self.links.start(
                self.held.at[k - 1], self.held.at[k + 2], self.ahead(k)
            )

    def total(self):
        total = self.part(0)
        for k in FAR:
            self.links.landed(self.tickets[k], self.held.at[k + 2])
            total = total + self.held[k + 2].astype(F32)
        return total


def kernel(
    slot_tile, land, feat_in, cot_in, dw_in, dw_bias_in, gain_in, shift_in, w_in, b_in_in, w_out_in,
    b_out_in, scale_in,
    out, gin, gout,
    feat, cot, dw, dw_bias, gain, shift, b_in, b_out, scale,
    xpad, cacc, hbuf, hsel, hsend, hrecv, hacc, wbuf, sbuf, dbuf0, dbuf1, nbuf, pre, qbuf, hid, back,
    gacc, gsend, gcore, gx, gown, gz, mx, mown, mzs, mzr,
    load_sems, send_sems, recv_sems,
):
    place, links = Place(), Links(send_sems, recv_sems)
    core, zl = place.core, place.zl
    first = place.space * 2
    barrier = pltpu.get_barrier_semaphore()
    for peer in place.peers():
        pl.semaphore_signal(barrier, inc=1, device_id=peer, device_id_type=MESH)
    loads = {}
    for name, source, target in (
        ("feat", feat_in, feat),
        ("scale", scale_in, scale),
        ("cot", cot_in, cot),
        ("w_in", w_in, wbuf.at[place.space, 0]),
        ("w_out", w_out_in, wbuf.at[place.space, 1]),
        ("dw", dw_in, dw),
        ("dw_bias", dw_bias_in, dw_bias),
        ("gain", gain_in, gain),
        ("shift", shift_in, shift),
        ("b_in", b_in_in, b_in),
        ("b_out", b_out_in, b_out),
    ):
        loads[name] = pltpu.make_async_copy(source, target, load_sems.at[len(loads)])
        loads[name].start()

    xpad[...] = jnp.zeros((2, 22, 32, 128), F32)
    hacc[...] = jnp.zeros((2, 2, 3, 32, 128), F32)
    tiles = [slot_tile[first + t] for t in range(2)]
    lands = [land[tile].astype(F32) for tile in tiles]
    loads["feat"].wait()
    for t in range(2):
        masked = feat[t * 256 : (t + 1) * 256, :].astype(F32) * lands[t]
        xpad[t, 3:19, 8:24, :] = masked.reshape(16, 16, 128)
        for side, begin in ((0, 0), (1, 13)):
            for q in range(3):
                column = xpad[t, 3:19, 8 + begin + q, :]
                hbuf[0, t * 2 + side, q] = column.astype(BF16)
    pl.semaphore_wait(barrier, len(place.peers()))

    dests = [(d, other) for other in (False, True) for d in range(4)]
    wanted = [
        [slot_tile[place.slot(dx=d, other=other) * 2 + t] for t in range(2)] for d, other in dests
    ]

    def pick(k):
        held = [slot_tile[place.slot(dz=-k) * 2 + i] for i in range(2)]
        strips = [hbuf[k, i].astype(F32) for i in range(4)]
        for n in range(8):
            for t in range(2):
                for side, step in ((0, -1), (1, 1)):
                    chosen = [(held[i] == wanted[n][t] + step).astype(F32) for i in range(2)]
                    found = strips[1 - side] * chosen[0] + strips[3 - side] * chosen[1]
                    if k:
                        found = found + hsel[n, t, side]
                    hsel[n, t, side] = found

    weights = SpaceGather(links, place, lambda s: wbuf.at[s])
    slopes = ChanGather(links, place, lambda c: sbuf.at[c])
    dbufs = (dbuf0, dbuf1)
    convs = [
        kind(links, place, lambda c, held=held: held.at[c])
        for kind, held in zip((ChanGather, ChanGatherY), dbufs)
    ]

    halo_z = {d: links.start(hbuf.at[0], hbuf.at[d], place.ahead_z(d)) for d in FAR}
    loads["scale"].wait()
    loads["cot"].wait()
    for t in range(2):
        rows = slice(t * 256, (t + 1) * 256)
        sbuf[place.chan, rows] = (cot[rows, :].astype(F32) * lands[t] * scale[...]).astype(BF16)
    slopes.own_y()
    slopes.own_zl()
    for name in ("w_in", "w_out"):
        loads[name].wait()
    weights.spread(0)
    pick(0)

    for name in ("dw", "dw_bias"):
        loads[name].wait()

    def inner(n, carry):
        t, i = n // 2, n % 2
        total = jnp.zeros((8, 16, 128), F32) + dw_bias[...][None]
        for e in range(7):
            rows = xpad[t, pl.ds(i * 8, 14), 5 + e : 21 + e, :]
            for a in range(7):
                total = total + dw[a, e : e + 1, :][None] * rows[a : a + 8]
        cacc[t, pl.ds(i * 8, 8)] = total
        return carry

    lax.fori_loop(0, 4, inner, 0)
    for d in FAR:
        links.landed(halo_z[d], hbuf.at[d])
        pick(d)
    halo_x = {}
    for n in (5, 7, 1, 3, 6, 2, 4):
        d, other = dests[n]
        hsend[n] = hsel[n].astype(BF16)
        device = place.across(d) if other else place.ahead_x(d)
        halo_x[n] = links.start(hsend.at[n], hrecv.at[n], device)
    slopes.cross()
    weights.own_z()
    for t in range(2):
        for side in range(2):
            hacc[t, side, :, 8:24] = hsel[0, t, side]
    for n, ticket in halo_x.items():
        links.landed(ticket, hrecv.at[n])
        for t in range(2):
            for side in range(2):
                hacc[t, side, :, 8:24] += hrecv[n, t, side].astype(F32)

    for t in range(2):
        for side in range(2):
            for q in range(3):
                total = jnp.zeros((16, 128), F32)
                for j in range(q, 3) if side == 0 else range(q + 1):
                    e = j - q if side == 0 else 6 + j - q
                    for a in range(7):
                        total = total + dw[a, e : e + 1, :] * hacc[t, side, j, 5 + a : 21 + a]
                cacc[t, :, 13 * side + q, :] += total
        dbufs[t][place.chan] = cacc[t].reshape(256, 128).astype(BF16)
        if t:
            convs[t].own_y()
            convs[t].own_zl()
        else:
            convs[t].own_zl()
            convs[t].own_y()

    for d in (1, 3):
        weights.spread(d)
    convs[0].cross()
    weights.spread(2)
    convs[1].cross()
    for d in (0,) + FAR:
        for e in FAR:
            weights.cross(d, e)
    slopes.wait()
    weights.wait()
    for name in ("gain", "shift", "b_in", "b_out"):
        loads[name].wait()

    for t in range(2):
        rows = slice(t * 256, (t + 1) * 256)
        slope_rows = jnp.concatenate([sbuf[c, rows] for c in range(8)], axis=1)
        qbuf[rows] = jnp.dot(
            slope_rows, wbuf[:, 1].reshape(1024, 512), preferred_element_type=F32
        )

    for t in range(2):
        convs[t].wait()

        def norm(i, carry):
            at = pl.ds(pl.multiple_of(i * 64, 64), 64)
            x = dbufs[t][:, at, :].astype(F32)
            mean = jnp.sum(jnp.sum(x, axis=0), axis=1, keepdims=True) * (1.0 / 1024)
            x = x - mean[None]
            spread = jnp.sum(jnp.sum(x * x, axis=0), axis=1, keepdims=True) * (1.0 / 1024)
            x = x * lax.rsqrt(spread + 1e-06)[None]
            to = pl.ds(pl.multiple_of(t * 256 + i * 64, 64), 64)
            for c in range(8):
                y = x[c] * gain[c : c + 1] + shift[c : c + 1]
                nbuf[to, c * 128 : (c + 1) * 128] = y.astype(BF16)
            return carry

        lax.fori_loop(0, 4, norm, 0)
        rows = slice(t * 256, (t + 1) * 256)
        pre[...] = (
            jnp.dot(nbuf[rows], wbuf[:, 0].reshape(1024, 512), preferred_element_type=F32)
            + b_in[...]
        )

        def act(i, carry):
            at = pl.ds(pl.multiple_of(i * 32, 32), 32)
            to = pl.ds(pl.multiple_of(t * 256 + i * 32, 32), 32)
            p = pre[at]
            below = 0.5 * (1.0 + lax.erf(p * 0.7071067811865476))
            hid[to] = (p * below).astype(BF16)
            rise = below + p * jnp.exp(-0.5 * p * p) * 0.3989422804014327
            back[to] = (qbuf[to] * rise).astype(BF16)
            return carry

        lax.fori_loop(0, 8, act, 0)

    over_core = {}
    for g in (1, 0):
        for i in range(4):
            if g:
                left = jnp.concatenate((sbuf[2 * i], sbuf[2 * i + 1]), axis=1)
            else:
                left = nbuf[:, i * 256 : (i + 1) * 256]
            summed = lax.dot_general(
                left, (hid if g else back)[...], (((0,), (0,)), ((), ())),
                preferred_element_type=F32,
            )
            gacc[g, 4 * i : 4 * i + 4] = summed.reshape(4, 2, 32, 512)
            gsend[g, 4 * i : 4 * i + 4] = gacc[g, 4 * i : 4 * i + 4, 1 - core].astype(BF16)
        for k in (2, 1, 3, 0):
            at = pl.ds(wrap4(place.x + k) * 4, 4)
            over_core[g, k] = links.start(gsend.at[g, at], gcore.at[g, at], place.other_core())

    def grad_part(g):
        def part(k, h):
            at = pl.ds(wrap4(place.x + k) * 4 + 2 * h, 2)
            return gacc[g, at, core] + gcore[g, at].astype(F32)

        return part

    over_x = [RingSum(links, place.ahead_x, grad_part(g), gx.at[g]) for g in range(2)]
    over_z = [
        DirectSum(
            links, place.ahead_z, lambda k, g=g: gown[g, wrap4(place.zh + k)], gz.at[g]
        )
        for g in range(2)
    ]
    for g in (1, 0):
        for k in (2, 1, 3, 0):
            links.landed(over_core[g, k], gcore.at[g, pl.ds(wrap4(place.x + k) * 4, 4)])
            if k == 2:
                over_x[g].far()
        if g:
            over_x[g].near()

    for k in (2, 1, 3, 0):
        to = wrap4(place.y + k)
        columns = jnp.concatenate(
            [wbuf[pl.ds(i * 16 + to * 4, 4), 1].reshape(128, 512) for i in range(2)], axis=0
        )
        partial = lax.dot_general(
            hid[...], columns, (((1,), (1,)), ((), ())), preferred_element_type=F32
        )
        for t in range(2):
            for i in range(2):
                mown[k, t, i] = partial[t * 256 : (t + 1) * 256, i * 128 : (i + 1) * 128]
    over_y = RingSum(links, place.ahead_y, lambda k, h: mown[k, h], mx)
    over_y.far()
    over_y.near()
    over_x[1].relay()
    over_x[0].near()
    over_x[0].relay()
    for g in (1, 0):
        for h in range(2):
            gown[g, 2 * h : 2 * h + 2] = over_x[g].total(h)
        over_z[g].start()
        if g:
            over_y.relay()
    for t in range(2):
        mown[0, t] = over_y.total(t)
        mzs[t] = mown[0, t, 1 - zl].astype(BF16)
    mixed_z = links.start(mzs, mzr, place.other_zl())
    links.landed(mixed_z, mzr)
    for t in range(2):
        rows = slice(t * 256, (t + 1) * 256)
        mixed = mown[0, t, zl] + mzr[t].astype(F32)
        value = feat[rows, :].astype(F32) + scale[...] * (mixed + b_out[...])
        out[rows, :] = (lands[t] * value).astype(BF16)
    for g, result in ((1, gout), (0, gin)):
        result[...] = over_z[g].total()
    links.finish()


def body(
    features, slot_tile, land, dw_kernel, dw_bias, ln_gain, ln_bias, w_in, b_in, w_out, b_out,
    layer_scale, cotangent,
):
    vmem = pl.BlockSpec(memory_space=pltpu.VMEM)
    smem = pl.BlockSpec(memory_space=pltpu.SMEM)
    scratch = [
        ((512, 128), BF16),
        ((512, 128), BF16),
        ((7, 7, 128), F32),
        ((1, 128), F32),
        ((8, 128), F32),
        ((8, 128), F32),
        ((1, 512), F32),
        ((1, 128), F32),
        ((1, 128), F32),
        ((2, 22, 32, 128), F32),
        ((2, 16, 16, 128), F32),
        ((4, 4, 3, 16, 128), BF16),
        ((8, 2, 2, 3, 16, 128), F32),
        ((8, 2, 2, 3, 16, 128), BF16),
        ((8, 2, 2, 3, 16, 128), BF16),
        ((2, 2, 3, 32, 128), F32),
        ((32, 2, 32, 512), BF16),
        ((8, 512, 128), BF16),
        ((8, 256, 128), BF16),
        ((8, 256, 128), BF16),
        ((512, 1024), BF16),
        ((256, 512), F32),
        ((512, 512), F32),
        ((512, 512), BF16),
        ((512, 512), BF16),
        ((2, 16, 2, 32, 512), F32),
        ((2, 16, 32, 512), BF16),
        ((2, 16, 32, 512), BF16),
        ((2, 12, 2, 32, 512), BF16),
        ((2, 4, 32, 512), F32),
        ((2, 6, 32, 512), BF16),
        ((12, 2, 256, 128), BF16),
        ((4, 2, 2, 256, 128), F32),
        ((2, 256, 128), BF16),
        ((2, 256, 128), BF16),
    ]
    output, grad_in, grad_out = pl.pallas_call(
        kernel,
        out_shape=(
            jax.ShapeDtypeStruct((512, 128), BF16),
            jax.ShapeDtypeStruct((32, 512), F32),
            jax.ShapeDtypeStruct((32, 512), F32),
        ),
        in_specs=[smem, smem] + [pl.BlockSpec(memory_space=pltpu.HBM)] * 11,
        out_specs=(vmem, vmem, vmem),
        scratch_shapes=[pltpu.VMEM(shape, dtype) for shape, dtype in scratch]
        + [pltpu.SemaphoreType.DMA((11,)), pltpu.SemaphoreType.DMA((COPIES,)), pltpu.SemaphoreType.DMA((COPIES,))],
        compiler_params=pltpu.CompilerParams(
            collective_id=0, has_side_effects=True, vmem_limit_bytes=60 * 2**20
        ),
        name="block",
    )(
        slot_tile,
        land,
        features.reshape(512, 128),
        cotangent.reshape(512, 128),
        dw_kernel,
        dw_bias.reshape(1, 128),
        ln_gain.reshape(8, 128),
        ln_bias.reshape(8, 128),
        w_in,
        b_in.reshape(1, 512),
        w_out.T,
        b_out.reshape(1, 128),
        layer_scale.reshape(1, 128),
    )
    return output.reshape(features.shape), grad_in, grad_out.T


def solution(mesh):
    return jax.shard_map(
        body,
        mesh=mesh,
        in_specs=(
            P("space", None, None, "chan"),
            P(),
            P(),
            P(None, None, "chan"),
            P("chan"),
            P(),
            P(),
            P("space", "chan"),
            P("chan"),
            P("chan", "space"),
            P("chan"),
            P("chan"),
            P("space", None, None, "chan"),
        ),
        out_specs=(P("space", None, None, "chan"), P("space", "chan"), P("chan", "space")),
        check_vma=False,
    )
```
